512 devices in a mesh: exp: 16 (over x, z_lo), rep: 4 (over z_hi, core), tk: 8 (over y).
Axes of the slice: x: 4, y: 8, z: 8 (z_hi: 2, z_lo: 4; z = z_hi * 4 + z_lo), core: 2. Of those that a mesh axis runs over, the one named last changes fastest.
Arguments:
- hidden_input_rows: bfloat16 [8192, 2048], P(('exp', 'rep', 'tk')), may hold values from -6 to 6
- queries: bfloat16 [8192, 2048], P(('exp', 'rep', 'tk')), may hold values from -300 to 300
- new_keys: bfloat16 [8192, 512], P(('exp', 'rep', 'tk')), may hold values from -8 to 8
- new_values: bfloat16 [8192, 512], P(('exp', 'rep', 'tk')), may hold values from -6 to 6
- cache_keys: bfloat16 [8192, 64, 512], P(('exp', 'rep', 'tk')), may hold values from -8 to 8
- cache_values: bfloat16 [8192, 64, 512], P(('exp', 'rep', 'tk')), may hold values from -6 to 6
- cache_lengths: int32 [8192], P(('exp', 'rep', 'tk')), may hold values from 1 to 64, as said below
- moe_gain: bfloat16 [2048], replicated, may hold values from 0.099609375 to 1.8984375
- expert_ids: int32 [8192, 8], P(('exp', 'rep', 'tk')), may hold values from 0 to 127, as said below
- routing_weights: bfloat16 [8192, 8], P(('exp', 'rep', 'tk')), may hold values from 0.049804688 to 1
- expert_gate: bfloat16 [128, 2048, 768], P(('exp', 'tk'), None, 'rep'), may hold values from -0.125 to 0.125
- expert_up: bfloat16 [128, 2048, 768], P(('exp', 'tk'), None, 'rep'), may hold values from -0.125 to 0.125
- expert_down: bfloat16 [128, 2048, 768], P(('exp', 'tk'), None, 'rep'), may hold values from -0.21875 to 0.21875
- prev_hidden: bfloat16 [8192, 2048], P(('exp', 'rep', 'tk')), may hold values from -6 to 6
- talker_gain: bfloat16 [2048], replicated, may hold values from 0.099609375 to 1.8984375
- talker_proj: bfloat16 [2048, 1024], P(None, 'tk'), may hold values from -0.125 to 0.125
Outputs:
- layer_out: bfloat16 [8192, 2048], P(('exp', 'rep', 'tk'))
- talker_in: bfloat16 [8192, 1024], P(('exp', 'rep'), 'tk')
The draws below stay inside these ranges and needn't reach their ends.
Inputs may be any that keep to these rules, and one draw needn't show every extreme that they name: `cache_lengths`: the first row of every device has all 64 positions valid. `expert_ids`: the 8 experts of a row differ. The rows of one device name no expert more than 2 times; some expert is named exactly 2 times by the rows of every device.
All inputs are finite; a program needn't handle non-finite values.
Results may differ from the reference program's by a relative error of at most 0.015.
Values may be sent and summed in bfloat16 or wider, within the bound.
No kernel may reach another device: no remote copies, remote signals or barrier semaphores. Data moves between devices by JAX's collectives and lax.ppermute only.
A program may use at most 64 MiB of HBM per device.

```python
import math
import jax
import jax.numpy as jnp
from jax import lax

D = 2048
INNER = 768
HD = 128
KVH = 4
TD = 1024
TOPK = 8
ROW_DEV = 16
CACHE = 64
QH = 16
EXPERTS = 128
HGROUP = 192
CAP = 2
ROWS = 8192
N_REP = 4


def shared_keys(key):
    cached = jax.random.normal(jax.random.fold_in(key, 11), (ROWS, CACHE, KVH, HD), jnp.float32)
    return cached


def draw_cache_keys(key, part):
    cached = shared_keys(key)
    return cached.reshape(ROWS, CACHE, KVH * HD).astype(jnp.bfloat16)


def draw_queries(key, part):
    key = jax.random.fold_in(key, 2)
    fresh = jax.random.normal(key, (ROWS, KVH, QH // KVH, HD), jnp.float32)
    return fresh.reshape(ROWS, QH * HD).astype(jnp.bfloat16)


def draw_new_keys(key, part):
    key = jax.random.fold_in(key, 3)
    fresh = jax.random.normal(key, (ROWS, KVH, HD), jnp.float32)
    return fresh.reshape(ROWS, KVH * HD).astype(jnp.bfloat16)


def draw_cache_lengths(key, part):
    key = jax.random.fold_in(key, 4)
    drawn = jax.random.randint(key, (ROWS,), 1, CACHE + 1, jnp.int32)
    return jnp.where(jnp.arange(ROWS) % ROW_DEV == 0, CACHE, drawn).astype(jnp.int32)


def draw_expert_ids(key, part):
    key = jax.random.fold_in(key, 5)
    blocks = ROWS // ROW_DEV
    hottest = jax.random.randint(jax.random.fold_in(key, 1), (), 0, EXPERTS, jnp.int32)
    block_keys = jax.random.split(jax.random.fold_in(key, 2), blocks)

    def shuffled(block_key):
        return jax.random.permutation(block_key, EXPERTS).astype(jnp.int32)
    orders = jax.vmap(shuffled)(block_keys)
    second = orders[:, 1:2]
    orders = jnp.where(orders == hottest, second, orders)
    orders = orders.at[:, 1].set(hottest)
    allowed = int(ROW_DEV * TOPK // CAP < EXPERTS)
    shifts = jax.random.randint(jax.random.fold_in(key, 3), (blocks, 1, 1), 0, 2, jnp.int32) * allowed
    position = jnp.arange(TOPK, dtype=jnp.int32)[None, :] * ROW_DEV + jnp.arange(ROW_DEV, dtype=jnp.int32)[:, None]
    quota = (position[None, :, :] + shifts) // CAP

    def pick(sorted_order, places):
        return sorted_order[places]
    chosen = jax.vmap(pick)(orders, quota)
    return chosen.reshape(ROWS, TOPK).astype(jnp.int32)


def shard_levels(own_key, extent, cuts, smallest, largest):
    def one(dim, blocks):
        heights = jax.random.uniform(jax.random.fold_in(jax.random.fold_in(own_key, 6), dim), (blocks,), jnp.float32, smallest / len(cuts), largest / len(cuts))
        return jnp.repeat(jnp.exp(heights), extent[dim] // blocks).reshape((-1,) + (1,) * (len(extent) - dim - 1))

    level = one(*cuts[0])
    for cut in cuts[1:]:
        level = level * one(*cut)
    return level


def bell_draw(rng, dims, scale, most, cuts=(), kind=jnp.bfloat16):
    values = jax.random.normal(rng, dims, jnp.float32) * scale
    if len(cuts) > 0:
        values = shard_levels(rng, dims, cuts, -0.22, 0.18) * values
    return jnp.clip(values, min=-most, max=most).astype(kind)


def setup_inputs(seed: int = 0) -> dict:
    seeds = jax.random.split(jax.random.key(seed), 17)
    return {
        "hidden_input_rows": bell_draw(seeds[0], (ROWS, D), 1.0, 6.0, ((0, 512),)),
        "queries": draw_queries(jax.random.fold_in(seeds[16], 71), 0),
        "new_keys": draw_new_keys(jax.random.fold_in(seeds[16], 71), 0),
        "new_values": bell_draw(seeds[3], (ROWS, KVH * HD), 1.0, 6.0, ((0, 512),)),
        "cache_keys": draw_cache_keys(jax.random.fold_in(seeds[16], 71), 0),
        "cache_values": bell_draw(seeds[5], (ROWS, CACHE, KVH * HD), 1.0, 6.0, ((0, 512),)),
        "cache_lengths": draw_cache_lengths(jax.random.fold_in(seeds[16], 71), 0),
        "moe_gain": jnp.clip(1.0 + 0.18 * jax.random.normal(seeds[7], (D,), jnp.float32), 0.099609375, 1.8984375).astype(jnp.bfloat16),
        "expert_ids": draw_expert_ids(jax.random.fold_in(seeds[16], 71), 0),
        "routing_weights": jnp.clip(jnp.exp(math.log(1.0) - 2.9996462 * jax.random.uniform(seeds[9], (ROWS, TOPK), jnp.float32) ** shard_levels(seeds[9], (ROWS, TOPK), ((0, 512),), -0.2, 0.2)), 0.049804688, 1.0).astype(jnp.bfloat16),
        "expert_gate": bell_draw(seeds[10], (EXPERTS, D, INNER), D ** -0.5, 0.125, ((0, 128), (2, 4))),
        "expert_up": bell_draw(seeds[11], (EXPERTS, D, INNER), D ** -0.5, 0.125, ((0, 128), (2, 4))),
        "expert_down": bell_draw(seeds[12], (EXPERTS, D, INNER), INNER ** -0.5, 0.21875, ((0, 128), (2, 4))),
        "prev_hidden": bell_draw(seeds[13], (ROWS, D), 1.0, 6.0, ((0, 512),)),
        "talker_gain": jnp.clip(1.0 + 0.18 * jax.random.normal(seeds[14], (D,), jnp.float32), 0.099609375, 1.8984375).astype(jnp.bfloat16),
        "talker_proj": bell_draw(seeds[15], (D, TD), D ** -0.5, 0.125, ((1, 8),)),
    }


def normalize(values, gain):
    wide = values.astype(jnp.float32)
    return wide * lax.rsqrt(lax.optimization_barrier(jnp.mean(wide * wide, axis=-1, keepdims=True)) + 1e-06) * gain.astype(jnp.float32)

def attend(queries, new_keys, new_values, cache_keys, cache_values, cache_lengths):
    count = queries.shape[0]
    span = cache_keys.shape[1]
    query_vector = queries.astype(jnp.float32).reshape(count, KVH, -1, HD)
    keys = cache_keys.astype(jnp.float32).reshape(count, span, KVH, HD)
    values = cache_values.astype(jnp.float32).reshape(count, span, KVH, HD)
    newest_key_row = new_keys.astype(jnp.float32).reshape(count, KVH, HD)
    fresh_value = new_values.astype(jnp.float32).reshape(count, KVH, HD)
    attention_scale = HD ** (-0.5)
    cached = jnp.einsum('bkgd,bjkd->bkgj', query_vector, keys) * attention_scale
    local_owned = jnp.einsum('crno,cro->crn', query_vector, newest_key_row) * attention_scale
    valid = (jnp.arange(span, dtype=jnp.int32)[None, :] < cache_lengths[:, None])[:, None, None, :]
    top = jnp.maximum(lax.optimization_barrier(jnp.max(jnp.where(valid, cached, -jnp.inf), axis=-1)), local_owned)
    weight_cache = jnp.where(valid, jnp.exp(cached - top[..., None]), 0.0)
    owned_weight = jnp.exp(local_owned - top)
    total = lax.optimization_barrier(jnp.sum(weight_cache, axis=-1)) + owned_weight
    prob_cache = (weight_cache / total[..., None]).astype(jnp.bfloat16)
    prob_own = (owned_weight / total).astype(jnp.bfloat16)
    mixed = jnp.einsum('bkgj,bjkd->bkgd', prob_cache.astype(jnp.float32), values)
    mixed = mixed + prob_own.astype(jnp.float32)[..., None] * fresh_value[:, :, None, :]
    return mixed.reshape(count, -1)

def reference(hidden_input_rows, queries, new_keys, new_values, cache_keys, cache_values, cache_lengths, moe_gain, expert_ids, routing_weights, expert_gate, expert_up, expert_down, prev_hidden, talker_gain, talker_proj):
    blocks = ROWS // ROW_DEV

    def split_rows(array):
        return array.reshape((blocks, ROW_DEV) + array.shape[1:])

    def attend_block(parts):
        return attend(*parts)
    attended = lax.map(attend_block, (split_rows(queries), split_rows(new_keys), split_rows(new_values), split_rows(cache_keys), split_rows(cache_values), split_rows(cache_lengths)))
    attended = attended.reshape(ROWS, -1)
    residual = hidden_input_rows.astype(jnp.float32) + attended
    moe_in = normalize(residual, moe_gain).astype(jnp.bfloat16)
    hits = expert_ids[:, :, None] == jnp.arange(EXPERTS, dtype=jnp.int32)[None, None, :]
    dense = lax.optimization_barrier(jnp.sum(jnp.where(hits, routing_weights.astype(jnp.float32)[:, :, None], 0.0), axis=1))
    capacity = CAP * blocks

    def one_expert(carry, expert):
        column = jnp.take(dense, expert, axis=1)
        picked = jnp.nonzero(column > 0, size=capacity, fill_value=ROWS)[0]
        chosen = jnp.take(moe_in, picked, axis=0, mode='clip')
        share = jnp.take(column, picked, mode='clip')
        gated = jnp.dot(chosen, expert_gate[expert], preferred_element_type=jnp.float32)
        raised = jnp.dot(chosen, expert_up[expert], preferred_element_type=jnp.float32)
        active = (jax.nn.silu(gated) * raised).astype(jnp.bfloat16)
        down = expert_down[expert]
        summed = jnp.zeros((capacity, D), jnp.float32)
        for group in range(N_REP):
            lower = group * HGROUP
            piece = jnp.dot(active[:, lower:lower + HGROUP], down[:, lower:lower + HGROUP].T, preferred_element_type=jnp.float32)
            piece = lax.optimization_barrier(piece.astype(jnp.bfloat16)).astype(jnp.float32)
            summed = summed + piece
        carry = carry.at[picked].add(share[:, None] * summed, mode='drop')
        return (carry, None)
    combined, _ = lax.scan(one_expert, jnp.zeros((ROWS, D), jnp.float32), jnp.arange(EXPERTS, dtype=jnp.int32))
    layer_out = (residual + combined).astype(jnp.bfloat16)
    talker_rows = normalize(prev_hidden, talker_gain).astype(jnp.bfloat16)
    talker_in = jnp.dot(talker_rows, talker_proj, preferred_element_type=jnp.float32).astype(jnp.bfloat16)
    return (layer_out, talker_in)
```

```python
import functools

import jax
import jax.numpy as jnp
from jax import lax
from jax.experimental import pallas as pl
from jax.experimental.pallas import tpu as pltpu
from jax.sharding import PartitionSpec as P

HD = 128
KVH = 4
AXES = ("exp", "rep", "tk")
NX, NZL, NZH, NY = 4, 4, 2, 8
NZ = NZL * NZH


def position(x, y, z, core):
    return ((x * NZL + z % NZL) * 2 * NZH + (z // NZL) * 2 + core) * NY + y


def line_groups():
    along_y = [[position(x, y, z, 0) for y in range(NY)] for x in range(NX) for z in range(NZ)]
    along_z = [[position(x, y, z, 1) for z in range(NZ)] for x in range(NX) for y in range(NY)]
    return along_y + along_z


def plane_groups():
    plane_xz = [[position(x, y, z, 0) for x in range(NX) for z in range(NZ)] for y in range(NY)]
    plane_xy = [[position(x, y, z, 1) for x in range(NX) for y in range(NY)] for z in range(NZ)]
    return plane_xz + plane_xy


def exchange(blocks, groups):
    return lax.all_to_all(
        blocks, AXES, split_axis=0, concat_axis=0, axis_index_groups=groups, tiled=True
    )


def normalize(values, gain):
    wide = values.astype(jnp.float32)
    return (
        wide
        * lax.rsqrt(jnp.mean(wide * wide, axis=-1, keepdims=True) + 1e-06)
        * gain.astype(jnp.float32)
    )


def attend(queries, new_keys, new_values, cache_keys, cache_values, cache_lengths):
    count = queries.shape[0]
    span = cache_keys.shape[1]
    query_vector = queries.reshape(count, KVH, -1, HD)
    keys = cache_keys.reshape(count, span, KVH, HD)
    values = cache_values.reshape(count, span, KVH, HD)
    newest_key_row = new_keys.reshape(count, KVH, HD)
    fresh_value = new_values.reshape(count, KVH, HD)
    attention_scale = HD ** (-0.5)
    cached = (
        jnp.einsum("bkgd,bjkd->bkgj", query_vector, keys, preferred_element_type=jnp.float32)
        * attention_scale
    )
    local_owned = (
        jnp.einsum(
            "crno,cro->crn", query_vector, newest_key_row, preferred_element_type=jnp.float32
        )
        * attention_scale
    )
    valid = (jnp.arange(span, dtype=jnp.int32)[None, :] < cache_lengths[:, None])[:, None, None, :]
    top = jnp.maximum(jnp.max(jnp.where(valid, cached, -jnp.inf), axis=-1), local_owned)
    weight_cache = jnp.where(valid, jnp.exp(cached - top[..., None]), 0.0)
    owned_weight = jnp.exp(local_owned - top)
    total = jnp.sum(weight_cache, axis=-1) + owned_weight
    prob_cache = (weight_cache / total[..., None]).astype(jnp.bfloat16)
    prob_own = (owned_weight / total).astype(jnp.bfloat16)
    mixed = jnp.einsum("bkgj,bjkd->bkgd", prob_cache, values, preferred_element_type=jnp.float32)
    mixed = (
        mixed
        + prob_own.astype(jnp.float32)[..., None] * fresh_value.astype(jnp.float32)[:, :, None, :]
    )
    return mixed.reshape(count, -1)


def dense_route(expert_ids, routing_weights, experts):
    hits = expert_ids[:, :, None] == jnp.arange(experts, dtype=jnp.int32)[None, None, :]
    spread = jnp.where(hits, routing_weights.astype(jnp.float32)[:, :, None], 0.0)
    return jnp.sum(spread, axis=1).astype(jnp.bfloat16)


def slot_masks(route, slots):
    rows, experts = route.shape
    exp, rep, tk = (lax.axis_index(a) for a in AXES)
    core, z_lo = rep % 2, exp % NZL
    target = lax.broadcasted_iota(jnp.int32, (NX * NZ, experts), 0)
    x, rest = target // NZ, target % NZ
    holds = jnp.where(core == 0, (x * NZL + rest % NZL) * NY + tk, (x * NZL + z_lo) * NY + rest)
    chosen = (holds == lax.broadcasted_iota(jnp.int32, holds.shape, 1)).astype(jnp.bfloat16)
    share = lax.dot_general(
        chosen, route, (((1,), (1,)), ((), ())), preferred_element_type=jnp.float32
    )
    member = share > 0
    before = lax.broadcasted_iota(jnp.int32, (rows, rows), 0)
    until = before <= lax.broadcasted_iota(jnp.int32, (rows, rows), 1)
    rank = jnp.dot(
        member.astype(jnp.bfloat16), until.astype(jnp.bfloat16), preferred_element_type=jnp.float32
    ).astype(jnp.int32)
    slot = lax.broadcasted_iota(jnp.int32, (target.shape[0], slots, rows), 1) + 1
    inside = jnp.logical_and(member[:, None, :], rank[:, None, :] == slot)
    pick = inside.astype(jnp.bfloat16).reshape(-1, rows)
    weight = jnp.where(inside, share[:, None, :], 0.0).astype(jnp.bfloat16).reshape(-1, rows)
    return pick, weight


def expert_kernel(x_ref, ga_ref, gb_ref, ua_ref, ub_ref, da_ref, db_ref, o_ref):
    x = x_ref[...]
    across = (((1,), (1,)), ((), ()))

    def hidden(gate_ref, up_ref):
        gated = lax.dot_general(x, gate_ref[...], across, preferred_element_type=jnp.float32)
        raised = lax.dot_general(x, up_ref[...], across, preferred_element_type=jnp.float32)
        return (gated / (1.0 + jnp.exp(-gated)) * raised).astype(jnp.bfloat16)

    near = hidden(ga_ref, ua_ref)
    far = hidden(gb_ref, ub_ref)
    out = jnp.dot(near, da_ref[...], preferred_element_type=jnp.float32)
    out = out + jnp.dot(far, db_ref[...], preferred_element_type=jnp.float32)
    o_ref[...] = out.astype(jnp.bfloat16)


def expert_apply(rows, weights):
    count, width = rows.shape
    block = 128
    whole = [pl.BlockSpec(w.shape, lambda i: (0, 0)) for w in weights]
    units = weights[0].shape[0]
    return pl.pallas_call(
        expert_kernel,
        grid=(count // block,),
        in_specs=[pl.BlockSpec((block, width), lambda i: (i, 0))] + whole,
        out_specs=pl.BlockSpec((block, width), lambda i: (i, 0)),
        out_shape=jax.ShapeDtypeStruct((count, width), jnp.bfloat16),
        compiler_params=pltpu.CompilerParams(vmem_limit_bytes=40 * 1024 * 1024),
        cost_estimate=pl.CostEstimate(
            flops=2 * count * width * units * 6,
            bytes_accessed=4 * count * width + 12 * units * width,
            transcendentals=2 * count * units,
        ),
        name="experts",
    )(rows, *weights)


def per_device(
    hidden_input_rows,
    queries,
    new_keys,
    new_values,
    cache_keys,
    cache_values,
    cache_lengths,
    moe_gain,
    expert_ids,
    routing_weights,
    expert_gate,
    expert_up,
    expert_down,
    prev_hidden,
    talker_gain,
    talker_proj,
):
    count, width = hidden_input_rows.shape
    experts = lax.axis_size("exp") * lax.axis_size("tk")
    lines, planes = line_groups(), plane_groups()

    other_core = [(r, r ^ 1) for r in range(2 * NZH)]
    weights = []
    for own in (expert_gate, expert_up, expert_down):
        own = own[0].T
        weights += [own, lax.ppermute(own, "rep", other_core)]

    attended = attend(queries, new_keys, new_values, cache_keys, cache_values, cache_lengths)
    residual = hidden_input_rows.astype(jnp.float32) + attended
    moe_in = normalize(residual, moe_gain).astype(jnp.bfloat16)
    route = dense_route(expert_ids, routing_weights, experts)

    sent = jnp.concatenate([moe_in, route], axis=1)
    line = len(lines[0])
    held = exchange(jnp.broadcast_to(sent[None], (line,) + sent.shape), lines)
    held = held.reshape(line * count, width + experts)
    slots = 2 * line
    pick, weight = slot_masks(held[:, width:], slots)
    outgoing = jnp.dot(pick, held[:, :width], preferred_element_type=jnp.float32)
    outgoing = outgoing.astype(jnp.bfloat16).reshape(-1, slots, width)
    arrived = exchange(outgoing, planes).reshape(-1, width)
    computed = expert_apply(arrived, weights)
    returned = exchange(computed.reshape(-1, slots, width), planes).reshape(-1, width)
    partial_rows = lax.dot_general(
        weight, returned, (((0,), (0,)), ((), ())), preferred_element_type=jnp.float32
    ).astype(jnp.bfloat16)
    pieces = exchange(partial_rows.reshape(line, count, width), lines)
    layer_out = (residual + jnp.sum(pieces.astype(jnp.float32), axis=0)).astype(jnp.bfloat16)

    talker_rows = normalize(prev_hidden, talker_gain).astype(jnp.bfloat16)
    talker_in = jnp.dot(
        lax.all_gather(talker_rows, "tk", axis=0, tiled=True),
        talker_proj,
        preferred_element_type=jnp.float32,
    ).astype(jnp.bfloat16)
    return (layer_out, talker_in)


def solution(mesh):
    placed = (
        P(("exp", "rep", "tk"), None),
        P(("exp", "rep", "tk"), None),
        P(("exp", "rep", "tk"), None),
        P(("exp", "rep", "tk"), None),
        P(("exp", "rep", "tk"), None, None),
        P(("exp", "rep", "tk"), None, None),
        P(("exp", "rep", "tk")),
        P(),
        P(("exp", "rep", "tk"), None),
        P(("exp", "rep", "tk"), None),
        P(("exp", "tk"), None, "rep"),
        P(("exp", "tk"), None, "rep"),
        P(("exp", "tk"), None, "rep"),
        P(("exp", "rep", "tk"), None),
        P(),
        P(None, "tk"),
    )
    return jax.shard_map(
        per_device,
        mesh=mesh,
        in_specs=placed,
        out_specs=(P(("exp", "rep", "tk"), None), P(("exp", "rep"), "tk")),
        check_vma=False,
    )
```

```python
import functools

import jax
import jax.numpy as jnp
from jax import lax
from jax.experimental import pallas as pl
from jax.experimental.pallas import tpu as pltpu
from jax.sharding import PartitionSpec as P

HD = 128
KVH = 4
BIG_VMEM = 60 * 1024 * 1024
SMALL_VMEM = 24 * 1024 * 1024
AXES = ("exp", "rep", "tk")
NX, NZL, NZH, NY = 4, 4, 2, 8
NZ = NZL * NZH


def position(x, y, z, core):
    return ((x * NZL + z % NZL) * 2 * NZH + (z // NZL) * 2 + core) * NY + y


def line_groups():
    along_y = [[position(x, y, z, 0) for y in range(NY)] for x in range(NX) for z in range(NZ)]
    along_z = [[position(x, y, z, 1) for z in range(NZ)] for x in range(NX) for y in range(NY)]
    return along_y + along_z


def plane_groups():
    plane_xz = [[position(x, y, z, 0) for x in range(NX) for z in range(NZ)] for y in range(NY)]
    plane_xy = [[position(x, y, z, 1) for x in range(NX) for y in range(NY)] for z in range(NZ)]
    return plane_xz + plane_xy


def exchange(blocks, groups):
    return lax.all_to_all(
        blocks, AXES, split_axis=0, concat_axis=0, axis_index_groups=groups, tiled=True
    )


def attend_kernel(
    lengths_ref,
    hidden_ref,
    q_ref,
    new_key_ref,
    new_value_ref,
    keys_ref,
    values_ref,
    gain_ref,
    ids_ref,
    routing_ref,
    sent_ref,
    residual_ref,
):
    count, span, _ = keys_ref.shape
    width = hidden_ref.shape[1]
    group = width // HD // KVH
    scale = HD ** (-0.5)
    row = lax.broadcasted_iota(jnp.int32, (count, count * span), 0)
    offset = lax.broadcasted_iota(jnp.int32, (count, count * span), 1) - row * span
    first = lax.broadcasted_iota(jnp.int32, (count, 1), 0)
    lengths = jnp.zeros((count, 1), jnp.int32)
    for r in range(count):
        lengths = jnp.where(first == r, lengths_ref[r], lengths)
    valid = jnp.logical_and(offset >= 0, offset < lengths)
    bias = jnp.concatenate([jnp.where(valid, 0.0, -1e30)] * group, axis=0)
    square = jnp.zeros((count, HD), jnp.float32)
    for head in range(KVH):
        lanes = [slice((head * group + h) * HD, (head * group + h + 1) * HD) for h in range(group)]
        query = jnp.concatenate([q_ref[:, lane] for lane in lanes], axis=0)
        own_lane = slice(head * HD, (head + 1) * HD)
        keys = keys_ref[:, :, own_lane].reshape(count * span, HD)
        values = values_ref[:, :, own_lane].reshape(count * span, HD)
        cached = lax.dot_general(
            query, keys, (((1,), (1,)), ((), ())), preferred_element_type=jnp.float32
        )
        cached = cached * scale + bias
        new_key = jnp.concatenate([new_key_ref[:, own_lane]] * group, axis=0).astype(jnp.float32)
        own = jnp.sum(query.astype(jnp.float32) * new_key, axis=-1, keepdims=True) * scale
        top = jnp.maximum(jnp.max(cached, axis=-1, keepdims=True), own)
        weight = jnp.exp(cached - top)
        own_weight = jnp.exp(own - top)
        share = 1.0 / (jnp.sum(weight, axis=-1, keepdims=True) + own_weight)
        probs = (weight * share).astype(jnp.bfloat16)
        own_prob = (own_weight * share).astype(jnp.bfloat16).astype(jnp.float32)
        mixed = jnp.dot(probs, values, preferred_element_type=jnp.float32)
        new_value = jnp.concatenate([new_value_ref[:, own_lane]] * group, axis=0)
        mixed = mixed + own_prob * new_value.astype(jnp.float32)
        for h, lane in enumerate(lanes):
            after = hidden_ref[:, lane].astype(jnp.float32) + mixed[h * count : (h + 1) * count]
            residual_ref[:, lane] = after
            square = square + after * after
    norm = lax.rsqrt(jnp.sum(square, axis=-1, keepdims=True) / width + 1e-06)
    gain = gain_ref[...].astype(jnp.float32).reshape(1, width)
    moe_in = (residual_ref[...] * norm * gain).astype(jnp.bfloat16)
    ids, routing = ids_ref[...], routing_ref[...].astype(jnp.float32)
    experts = sent_ref.shape[2] - width
    expert = lax.broadcasted_iota(jnp.int32, (experts, count), 0)
    route = jnp.zeros((experts, count), jnp.float32)
    for k in range(ids.shape[0]):
        route = route + jnp.where(expert == ids[k : k + 1], routing[k : k + 1], 0.0)
    route = route.T.astype(jnp.bfloat16)
    for copy in range(sent_ref.shape[0]):
        sent_ref[copy, :, :width] = moe_in
        sent_ref[copy, :, width:] = route


def origin(ndim, step):
    return (0,) * ndim


def attend(
    copies,
    experts,
    hidden,
    queries,
    new_keys,
    new_values,
    cache_keys,
    cache_values,
    lengths,
    gain,
    ids,
    routing,
):
    count, width = hidden.shape
    operands = (
        hidden,
        queries,
        new_keys,
        new_values,
        cache_keys,
        cache_values,
        gain,
        ids.T,
        routing.T,
    )
    return pl.pallas_call(
        attend_kernel,
        grid=(1,),
        in_specs=[pl.BlockSpec(memory_space=pltpu.SMEM)]
        + [pl.BlockSpec(o.shape, functools.partial(origin, o.ndim)) for o in operands],
        out_specs=[
            pl.BlockSpec((copies, count, width + experts), functools.partial(origin, 3)),
            pl.BlockSpec((count, width), functools.partial(origin, 2)),
        ],
        out_shape=[
            pltpu.HBM((copies, count, width + experts), jnp.bfloat16),
            jax.ShapeDtypeStruct((count, width), jnp.float32),
        ],
        compiler_params=pltpu.CompilerParams(vmem_limit_bytes=BIG_VMEM),
        name="attend",
    )(lengths, *operands)


def slot_masks(route, slots):
    rows, experts = route.shape
    exp, rep, tk = (lax.axis_index(a) for a in AXES)
    core, z_lo = rep % 2, exp % NZL
    target = lax.broadcasted_iota(jnp.int32, (NX * NZ, experts), 0)
    x, rest = target // NZ, target % NZ
    holds = jnp.where(core == 0, (x * NZL + rest % NZL) * NY + tk, (x * NZL + z_lo) * NY + rest)
    chosen = (holds == lax.broadcasted_iota(jnp.int32, holds.shape, 1)).astype(jnp.bfloat16)
    share = lax.dot_general(
        chosen, route, (((1,), (1,)), ((), ())), preferred_element_type=jnp.float32
    )
    member = share > 0
    before = lax.broadcasted_iota(jnp.int32, (rows, rows), 0)
    until = before <= lax.broadcasted_iota(jnp.int32, (rows, rows), 1)
    rank = jnp.dot(
        member.astype(jnp.bfloat16), until.astype(jnp.bfloat16), preferred_element_type=jnp.float32
    ).astype(jnp.int32)
    slot = lax.broadcasted_iota(jnp.int32, (target.shape[0], slots, rows), 1) + 1
    inside = jnp.logical_and(member[:, None, :], rank[:, None, :] == slot)
    pick = inside.astype(jnp.bfloat16).reshape(-1, rows)
    weight = jnp.where(inside, share[:, None, :], 0.0).astype(jnp.bfloat16).reshape(-1, rows)
    return pick, weight


def weight_pieces(units, block):
    pieces = []
    for first in range(0, 2 * units, block):
        for kind in range(2):
            unit = first
            while unit < first + block:
                side, row = divmod(unit, units)
                rows = min(first + block - unit, units - row)
                place = 2 * first + kind * block + unit - first
                pieces.append((2 * kind + side, row, rows, place))
                unit += rows
    return pieces


def expert_kernel(x_ref, *refs):
    weights, (o_ref, in_ref, down_ref, active_ref, out_ref, sems, out_sems) = refs[:6], refs[6:]
    units = weights[0].shape[0]
    block = 128
    pieces = weight_pieces(units, block)
    copies = [
        pltpu.make_async_copy(
            weights[array].at[pl.ds(row, rows)], in_ref.at[pl.ds(place, rows)], sems.at[i]
        )
        for i, (array, row, rows, place) in enumerate(pieces)
    ]
    down_copies = [
        pltpu.make_async_copy(
            weights[4 + i], down_ref.at[pl.ds(i * units, units)], sems.at[len(pieces) + i]
        )
        for i in range(2)
    ]
    for copy in copies + down_copies:
        copy.start()
    for first in range(0, 2 * units, block):
        for copy, piece in zip(copies, pieces):
            if 2 * first <= piece[3] < 2 * (first + block):
                copy.wait()
        both = lax.dot_general(
            x_ref[...],
            in_ref[2 * first : 2 * (first + block)],
            (((1,), (1,)), ((), ())),
            preferred_element_type=jnp.float32,
        )
        gated, raised = both[:, :block], both[:, block:]
        active_ref[:, first : first + block] = (
            gated / (1.0 + jnp.exp(-gated)) * raised
        ).astype(jnp.bfloat16)
    for copy in down_copies:
        copy.wait()
    parts, _, part = out_ref.shape
    out_copies = []
    for i in range(parts):
        lanes = pl.ds(i * part, part)
        out = jnp.dot(active_ref[...], down_ref[:, lanes], preferred_element_type=jnp.float32)
        out_ref[i] = out.astype(jnp.bfloat16)
        out_copies.append(pltpu.make_async_copy(out_ref.at[i], o_ref.at[:, lanes], out_sems.at[i]))
        out_copies[-1].start()
    for copy in out_copies:
        copy.wait()


def expert_apply(rows, weights):
    count, width = rows.shape
    units = weights[0].shape[0]
    parts = 4
    return pl.pallas_call(
        expert_kernel,
        in_specs=[pl.BlockSpec(memory_space=pltpu.VMEM)]
        + [pl.BlockSpec(memory_space=pltpu.HBM)] * 6,
        out_specs=pl.BlockSpec(memory_space=pltpu.HBM),
        out_shape=pltpu.HBM((count, width), jnp.bfloat16),
        scratch_shapes=[
            pltpu.VMEM((4 * units, width), jnp.bfloat16),
            pltpu.VMEM((2 * units, width), jnp.bfloat16),
            pltpu.VMEM((count, 2 * units), jnp.bfloat16),
            pltpu.VMEM((parts, count, width // parts), jnp.bfloat16),
            pltpu.SemaphoreType.DMA((16,)),
            pltpu.SemaphoreType.DMA((parts,)),
        ],
        compiler_params=pltpu.CompilerParams(vmem_limit_bytes=SMALL_VMEM),
        cost_estimate=pl.CostEstimate(
            flops=12 * count * width * units,
            bytes_accessed=4 * count * width + 12 * units * width,
            transcendentals=2 * count * units,
        ),
        name="experts",
    )(rows, *weights)


def per_device(
    hidden_input_rows,
    queries,
    new_keys,
    new_values,
    cache_keys,
    cache_values,
    cache_lengths,
    moe_gain,
    expert_ids,
    routing_weights,
    expert_gate,
    expert_up,
    expert_down,
    prev_hidden,
    talker_gain,
    talker_proj,
):
    count, width = hidden_input_rows.shape
    experts = lax.axis_size("exp") * lax.axis_size("tk")
    lines, planes = line_groups(), plane_groups()
    line = len(lines[0])

    sent, residual = attend(
        line,
        experts,
        hidden_input_rows,
        queries,
        new_keys,
        new_values,
        cache_keys,
        cache_values,
        cache_lengths,
        moe_gain,
        expert_ids,
        routing_weights,
    )

    wide = prev_hidden.astype(jnp.float32)
    unit = wide * lax.rsqrt(jnp.mean(wide * wide, axis=-1, keepdims=True) + 1e-06)
    talker_units = lax.all_gather(unit, "tk", axis=0, tiled=True)

    own = [w[0].T for w in (expert_gate, expert_up, expert_down)]
    sent, own = lax.optimization_barrier((sent, own))
    other = [lax.ppermute(w, "rep", [(r, r ^ 1) for r in range(2 * NZH)]) for w in own]
    held = exchange(sent, lines).reshape(line * count, width + experts)
    held, own, other = lax.optimization_barrier((held, own, other))
    slots = 2 * line
    pick, weight = slot_masks(held[:, width:], slots)
    outgoing = jnp.dot(pick, held[:, :width], preferred_element_type=jnp.float32)
    outgoing = outgoing.astype(jnp.bfloat16).reshape(-1, slots, width)
    arrived = exchange(outgoing, planes).reshape(-1, width)
    weights = [own[0], other[0], own[1], other[1], own[2], other[2]]
    computed = expert_apply(arrived, weights)
    returned = exchange(computed.reshape(-1, slots, width), planes).reshape(-1, width)
    partial_rows = lax.dot_general(
        weight, returned, (((0,), (0,)), ((), ())), preferred_element_type=jnp.float32
    ).astype(jnp.bfloat16)
    pieces = exchange(partial_rows.reshape(line, count, width), lines)
    layer_out = (residual + jnp.sum(pieces.astype(jnp.float32), axis=0)).astype(jnp.bfloat16)

    talker_rows = (talker_units * talker_gain.astype(jnp.float32)).astype(jnp.bfloat16)
    talker_in = jnp.dot(talker_rows, talker_proj, preferred_element_type=jnp.float32)
    return (layer_out, talker_in.astype(jnp.bfloat16))


def solution(mesh):
    placed = (
        P(("exp", "rep", "tk"), None),
        P(("exp", "rep", "tk"), None),
        P(("exp", "rep", "tk"), None),
        P(("exp", "rep", "tk"), None),
        P(("exp", "rep", "tk"), None, None),
        P(("exp", "rep", "tk"), None, None),
        P(("exp", "rep", "tk")),
        P(),
        P(("exp", "rep", "tk"), None),
        P(("exp", "rep", "tk"), None),
        P(("exp", "tk"), None, "rep"),
        P(("exp", "tk"), None, "rep"),
        P(("exp", "tk"), None, "rep"),
        P(("exp", "rep", "tk"), None),
        P(),
        P(None, "tk"),
    )
    return jax.shard_map(
        per_device,
        mesh=mesh,
        in_specs=placed,
        out_specs=(P(("exp", "rep", "tk"), None), P(("exp", "rep"), "tk")),
        check_vma=False,
    )
```

```python
import functools

import jax
import jax.numpy as jnp
from jax import lax
from jax.experimental import pallas as pl
from jax.experimental.pallas import tpu as pltpu
from jax.sharding import PartitionSpec as P

HD = 128
KVH = 4
BIG_VMEM = 61 * 1024 * 1024
SMALL_VMEM = 12 * 1024 * 1024
AXES = ("exp", "rep", "tk")
NX, NZL, NZH, NY = 4, 4, 2, 8
NZ = NZL * NZH


def position(x, y, z, core):
    return ((x * NZL + z % NZL) * 2 * NZH + (z // NZL) * 2 + core) * NY + y


def line_groups():
    along_y = [[position(x, y, z, 0) for y in range(NY)] for x in range(NX) for z in range(NZ)]
    along_z = [[position(x, y, z, 1) for z in range(NZ)] for x in range(NX) for y in range(NY)]
    return along_y + along_z


def plane_groups():
    plane_xz = [[position(x, y, z, 0) for x in range(NX) for z in range(NZ)] for y in range(NY)]
    plane_xy = [[position(x, y, z, 1) for x in range(NX) for y in range(NY)] for z in range(NZ)]
    return plane_xz + plane_xy


def exchange(blocks, groups):
    return lax.all_to_all(
        blocks, AXES, split_axis=0, concat_axis=0, axis_index_groups=groups, tiled=True
    )


def attend_kernel(
    lengths_ref,
    hidden_ref,
    q_ref,
    new_key_ref,
    new_value_ref,
    keys_ref,
    values_ref,
    gain_ref,
    ids_ref,
    routing_ref,
    previous_ref,
    talker_gain_ref,
    sent_ref,
    residual_ref,
    talker_ref,
):
    count, span, _ = keys_ref.shape
    width = hidden_ref.shape[1]
    group = width // HD // KVH
    scale = HD ** (-0.5)
    row = lax.broadcasted_iota(jnp.int32, (count, count * span), 0)
    offset = lax.broadcasted_iota(jnp.int32, (count, count * span), 1) - row * span
    first = lax.broadcasted_iota(jnp.int32, (count, 1), 0)
    lengths = jnp.zeros((count, 1), jnp.int32)
    for r in range(count):
        lengths = jnp.where(first == r, lengths_ref[r], lengths)
    valid = jnp.logical_and(offset >= 0, offset < lengths)
    bias = jnp.concatenate([jnp.where(valid, 0.0, -1e30)] * group, axis=0)
    square = jnp.zeros((count, HD), jnp.float32)
    for head in range(KVH):
        lanes = [slice((head * group + h) * HD, (head * group + h + 1) * HD) for h in range(group)]
        query = jnp.concatenate([q_ref[:, lane] for lane in lanes], axis=0)
        own_lane = slice(head * HD, (head + 1) * HD)
        keys = keys_ref[:, :, own_lane].reshape(count * span, HD)
        values = values_ref[:, :, own_lane].reshape(count * span, HD)
        cached = lax.dot_general(
            query, keys, (((1,), (1,)), ((), ())), preferred_element_type=jnp.float32
        )
        cached = cached * scale + bias
        new_key = jnp.concatenate([new_key_ref[:, own_lane]] * group, axis=0).astype(jnp.float32)
        own = jnp.sum(query.astype(jnp.float32) * new_key, axis=-1, keepdims=True) * scale
        top = jnp.maximum(jnp.max(cached, axis=-1, keepdims=True), own)
        weight = jnp.exp(cached - top)
        own_weight = jnp.exp(own - top)
        share = 1.0 / (jnp.sum(weight, axis=-1, keepdims=True) + own_weight)
        probs = (weight * share).astype(jnp.bfloat16)
        own_prob = (own_weight * share).astype(jnp.bfloat16).astype(jnp.float32)
        mixed = jnp.dot(probs, values, preferred_element_type=jnp.float32)
        new_value = jnp.concatenate([new_value_ref[:, own_lane]] * group, axis=0)
        mixed = mixed + own_prob * new_value.astype(jnp.float32)
        for h, lane in enumerate(lanes):
            after = hidden_ref[:, lane].astype(jnp.float32) + mixed[h * count : (h + 1) * count]
            residual_ref[:, lane] = after
            square = square + after * after
    norm = lax.rsqrt(jnp.sum(square, axis=-1, keepdims=True) / width + 1e-06)
    gain = gain_ref[...].astype(jnp.float32).reshape(1, width)
    moe_in = (residual_ref[...] * norm * gain).astype(jnp.bfloat16)
    ids, routing = ids_ref[...], routing_ref[...].astype(jnp.float32)
    experts = sent_ref.shape[2] - width
    expert = lax.broadcasted_iota(jnp.int32, (experts, count), 0)
    route = jnp.zeros((experts, count), jnp.float32)
    for k in range(ids.shape[0]):
        route = route + jnp.where(expert == ids[k : k + 1], routing[k : k + 1], 0.0)
    route = route.T.astype(jnp.bfloat16)
    for copy in range(sent_ref.shape[0]):
        sent_ref[copy, :, :width] = moe_in
        sent_ref[copy, :, width:] = route
    previous = previous_ref[...].astype(jnp.float32)
    norm = lax.rsqrt(jnp.mean(previous * previous, axis=-1, keepdims=True) + 1e-06)
    gain = talker_gain_ref[...].astype(jnp.float32).reshape(1, width)
    talker_ref[...] = (previous * norm * gain).astype(jnp.bfloat16)


def origin(ndim, step):
    return (0,) * ndim


def attend(
    copies,
    experts,
    hidden,
    queries,
    new_keys,
    new_values,
    cache_keys,
    cache_values,
    lengths,
    gain,
    ids,
    routing,
    previous,
    talker_gain,
):
    count, width = hidden.shape
    operands = (
        hidden,
        queries,
        new_keys,
        new_values,
        cache_keys,
        cache_values,
        gain,
        ids.T,
        routing.T,
        previous,
        talker_gain,
    )
    return pl.pallas_call(
        attend_kernel,
        grid=(1,),
        in_specs=[pl.BlockSpec(memory_space=pltpu.SMEM)]
        + [pl.BlockSpec(o.shape, functools.partial(origin, o.ndim)) for o in operands],
        out_specs=[
            pl.BlockSpec((copies, count, width + experts), functools.partial(origin, 3)),
            pl.BlockSpec((count, width), functools.partial(origin, 2)),
            pl.BlockSpec((count, width), functools.partial(origin, 2)),
        ],
        out_shape=[
            pltpu.HBM((copies, count, width + experts), jnp.bfloat16),
            jax.ShapeDtypeStruct((count, width), jnp.float32),
            pltpu.HBM((count, width), jnp.bfloat16),
        ],
        compiler_params=pltpu.CompilerParams(vmem_limit_bytes=BIG_VMEM),
        name="attend",
    )(lengths, *operands)


def from_row(values, ahead):
    return lax.ppermute(values, "tk", [((y + ahead) % NY, y) for y in range(NY)])


def dispatch_kernel(where_ref, held_ref, o_ref, weight_ref, out_ref, sems):
    core, tk, z_lo = where_ref[0], where_ref[1], where_ref[2]
    width = o_ref.shape[1]
    rows, experts = weight_ref.shape[0], held_ref.shape[1] - width
    targets = NX * NZ
    slots = weight_ref.shape[1] // targets
    across = (((1,), (1,)), ((), ()))

    def count(shape, axis):
        return lax.broadcasted_iota(jnp.int32, shape, axis)

    def bits(mask):
        return mask.astype(jnp.bfloat16)

    target = count((targets, experts), 0)
    x, rest = target // NZ, target % NZ
    holds = jnp.where(core == 0, (x * NZL + rest % NZL) * NY + tk, (x * NZL + z_lo) * NY + rest)
    chosen = bits(holds == count((targets, experts), 1))
    route = held_ref[:, width:]

    share = lax.dot_general(chosen, route, across, preferred_element_type=jnp.float32)
    until = bits(count((rows, rows), 0) <= count((rows, rows), 1))
    rank = jnp.dot(bits(share > 0), until, preferred_element_type=jnp.float32)
    rank = jnp.where(share > 0, rank, 0.0)
    shape = (targets, slots, rows)
    slot = count(shape, 1).astype(jnp.float32) + 1.0
    inside = jnp.broadcast_to(rank[:, None, :], shape) == slot
    pick = bits(jnp.where(inside, 1.0, 0.0).reshape(targets * slots, rows))
    parts, _, part = out_ref.shape
    copies = []
    for i in range(parts):
        lanes = pl.ds(i * part, part)
        out = jnp.dot(pick, held_ref[:, lanes], preferred_element_type=jnp.float32)
        out_ref[i] = out.astype(jnp.bfloat16)
        copies.append(pltpu.make_async_copy(out_ref.at[i], o_ref.at[:, lanes], sems.at[i]))
        copies[-1].start()

    share = lax.dot_general(route, chosen, across, preferred_element_type=jnp.float32)
    since = bits(count((rows, rows), 0) >= count((rows, rows), 1))
    rank = jnp.dot(since, bits(share > 0), preferred_element_type=jnp.float32)
    rank = jnp.where(share > 0, rank, 0.0)
    wide = (targets, targets * slots)
    repeat = bits(count(wide, 0) == count(wide, 1) // slots)
    rank = jnp.dot(rank.astype(jnp.bfloat16), repeat, preferred_element_type=jnp.float32)
    share = jnp.dot(share.astype(jnp.bfloat16), repeat, preferred_element_type=jnp.float32)
    slot = (count(rank.shape, 1) % slots).astype(jnp.float32) + 1.0
    weight_ref[...] = jnp.where(rank == slot, share, 0.0).astype(jnp.bfloat16)
    for copy in copies:
        copy.wait()


def dispatch(held, width, slots):
    rows = held.shape[0]
    count = NX * NZ * slots
    exp, rep, tk = (lax.axis_index(a) for a in AXES)
    where = jnp.stack([rep % 2, tk, exp % NZL]).astype(jnp.int32)
    parts = 4
    return pl.pallas_call(
        dispatch_kernel,
        in_specs=[
            pl.BlockSpec(memory_space=pltpu.SMEM),
            pl.BlockSpec(memory_space=pltpu.VMEM),
        ],
        out_specs=[
            pl.BlockSpec(memory_space=pltpu.HBM),
            pl.BlockSpec(memory_space=pltpu.VMEM),
        ],
        out_shape=[
            pltpu.HBM((count, width), jnp.bfloat16),
            jax.ShapeDtypeStruct((rows, count), jnp.bfloat16),
        ],
        scratch_shapes=[
            pltpu.VMEM((parts, count, width // parts), jnp.bfloat16),
            pltpu.SemaphoreType.DMA((parts,)),
        ],
        compiler_params=pltpu.CompilerParams(vmem_limit_bytes=SMALL_VMEM),
        name="dispatch",
    )(where, held)


def pack_kernel(*refs):
    weights, (packed_ref, sems) = refs[:-2], refs[-2:]
    units = weights[0].shape[0]
    copies = [
        pltpu.make_async_copy(w, packed_ref.at[pl.ds(i * units, units)], sems.at[i])
        for i, w in enumerate(weights)
    ]
    for copy in copies:
        copy.start()
    for copy in copies:
        copy.wait()


def pack(weights):
    units, width = weights[0].shape
    count = len(weights)
    return pl.pallas_call(
        pack_kernel,
        in_specs=[pl.BlockSpec(memory_space=pl.ANY)] * count,
        out_specs=pl.BlockSpec(memory_space=pltpu.HBM),
        out_shape=pltpu.HBM((count * units, width), jnp.bfloat16),
        scratch_shapes=[pltpu.SemaphoreType.DMA((count,))],
        compiler_params=pltpu.CompilerParams(vmem_limit_bytes=SMALL_VMEM),
        cost_estimate=pl.CostEstimate(
            flops=0, bytes_accessed=4 * count * units * width, transcendentals=0
        ),
        name="pack",
    )(*weights)


def expert_kernel(x_ref, packed_ref, o_ref, out_ref, sems):
    units = packed_ref.shape[0] // 3
    both = lax.dot_general(
        x_ref[...],
        packed_ref[: 2 * units],
        (((1,), (1,)), ((), ())),
        preferred_element_type=jnp.float32,
    )
    gated, raised = both[:, :units], both[:, units:]
    active = (gated / (1.0 + jnp.exp(-gated)) * raised).astype(jnp.bfloat16)
    parts, _, part = out_ref.shape
    copies = []
    for i in range(parts):
        lanes = pl.ds(i * part, part)
        out = jnp.dot(
            active, packed_ref[2 * units :, lanes], preferred_element_type=jnp.float32
        )
        out_ref[i] = out.astype(jnp.bfloat16)
        copies.append(pltpu.make_async_copy(out_ref.at[i], o_ref.at[:, lanes], sems.at[i]))
        copies[-1].start()
    for copy in copies:
        copy.wait()


def expert_apply(rows, packed):
    count, width = rows.shape
    units = packed.shape[0] // 3
    parts = 4
    return pl.pallas_call(
        expert_kernel,
        in_specs=[pl.BlockSpec(memory_space=pltpu.VMEM)] * 2,
        out_specs=pl.BlockSpec(memory_space=pltpu.HBM),
        out_shape=pltpu.HBM((count, width), jnp.bfloat16),
        scratch_shapes=[
            pltpu.VMEM((parts, count, width // parts), jnp.bfloat16),
            pltpu.SemaphoreType.DMA((parts,)),
        ],
        compiler_params=pltpu.CompilerParams(vmem_limit_bytes=SMALL_VMEM),
        cost_estimate=pl.CostEstimate(
            flops=6 * count * width * units,
            bytes_accessed=4 * count * width + 6 * units * width,
            transcendentals=count * units,
        ),
        name="experts",
    )(rows, packed)


def per_device(
    hidden_input_rows,
    queries,
    new_keys,
    new_values,
    cache_keys,
    cache_values,
    cache_lengths,
    moe_gain,
    expert_ids,
    routing_weights,
    expert_gate,
    expert_up,
    expert_down,
    prev_hidden,
    talker_gain,
    talker_proj,
):
    count, width = hidden_input_rows.shape
    experts = lax.axis_size("exp") * lax.axis_size("tk")
    lines, planes = line_groups(), plane_groups()
    line = len(lines[0])

    sent, residual, talker_rows = attend(
        line,
        experts,
        hidden_input_rows,
        queries,
        new_keys,
        new_values,
        cache_keys,
        cache_values,
        cache_lengths,
        moe_gain,
        expert_ids,
        routing_weights,
        prev_hidden,
        talker_gain,
    )

    near = [from_row(talker_rows, 1), from_row(talker_rows, -1)]
    held = exchange(sent, lines).reshape(line * count, width + experts)
    held, near = lax.optimization_barrier((held, near))
    slots = 2 * line
    outgoing, weight = dispatch(held, width, slots)

    own = [w[0].T for w in (expert_gate, expert_up, expert_down)]
    outgoing, own, near = lax.optimization_barrier((outgoing, own, near))
    other = [lax.ppermute(w, "rep", [(r, r ^ 1) for r in range(2 * NZH)]) for w in own]
    second = [from_row(near[0], 1), from_row(near[1], -1)]
    arrived = exchange(outgoing.reshape(-1, slots, width), planes).reshape(-1, width)
    packed = pack([own[0], other[0], own[1], other[1], own[2], other[2]])
    arrived, packed, second = lax.optimization_barrier((arrived, packed, second))
    computed = expert_apply(arrived, packed)

    computed, second = lax.optimization_barrier((computed, second))
    third = [from_row(second[0], 1), from_row(second[1], -1)]
    half = count // 2
    third += [from_row(second[0][:half], 2), from_row(second[1][half:], -2)]
    returned = exchange(computed.reshape(-1, slots, width), planes).reshape(-1, width)
    returned, third = lax.optimization_barrier((returned, third))
    partial_rows = jnp.dot(weight, returned, preferred_element_type=jnp.float32)
    partial_rows = partial_rows.astype(jnp.bfloat16)
    partial_rows, third = lax.optimization_barrier((partial_rows, third))
    pieces = exchange(partial_rows.reshape(line, count, width), lines)
    layer_out = (residual + jnp.sum(pieces.astype(jnp.float32), axis=0)).astype(jnp.bfloat16)

    ahead = [talker_rows, near[0], second[0], third[0], third[2], third[3]]
    gathered = jnp.concatenate(ahead + [third[1], second[1], near[1]], axis=0)
    talker_in = jnp.dot(gathered, talker_proj, preferred_element_type=jnp.float32)
    talker_in = talker_in.astype(jnp.bfloat16)
    start = (NY - lax.axis_index("tk")) * count
    talker_in = lax.dynamic_slice_in_dim(
        jnp.concatenate([talker_in, talker_in], axis=0), start, NY * count, axis=0
    )
    return (layer_out, talker_in)


def solution(mesh):
    placed = (
        P(("exp", "rep", "tk"), None),
        P(("exp", "rep", "tk"), None),
        P(("exp", "rep", "tk"), None),
        P(("exp", "rep", "tk"), None),
        P(("exp", "rep", "tk"), None, None),
        P(("exp", "rep", "tk"), None, None),
        P(("exp", "rep", "tk")),
        P(),
        P(("exp", "rep", "tk"), None),
        P(("exp", "rep", "tk"), None),
        P(("exp", "tk"), None, "rep"),
        P(("exp", "tk"), None, "rep"),
        P(("exp", "tk"), None, "rep"),
        P(("exp", "rep", "tk"), None),
        P(),
        P(None, "tk"),
    )
    return jax.shard_map(
        per_device,
        mesh=mesh,
        in_specs=placed,
        out_specs=(P(("exp", "rep", "tk"), None), P(("exp", "rep"), "tk")),
        check_vma=False,
    )
```

```python
import functools

import jax
import jax.numpy as jnp
from jax import lax
from jax.experimental import pallas as pl
from jax.experimental.pallas import tpu as pltpu
from jax.sharding import PartitionSpec as P

HD = 128
KVH = 4
BIG_VMEM = 61 * 1024 * 1024
SMALL_VMEM = 12 * 1024 * 1024
AXES = ("exp", "rep", "tk")
NX, NZL, NZH, NY = 4, 4, 2, 8
NZ = NZL * NZH


def position(x, y, z, core):
    return ((x * NZL + z % NZL) * 2 * NZH + (z // NZL) * 2 + core) * NY + y


def line_groups():
    along_y = [[position(x, y, z, 0) for y in range(NY)] for x in range(NX) for z in range(NZ)]
    along_z = [[position(x, y, z, 1) for z in range(NZ)] for x in range(NX) for y in range(NY)]
    return along_y + along_z


def plane_groups():
    plane_xz = [[position(x, y, z, 0) for x in range(NX) for z in range(NZ)] for y in range(NY)]
    plane_xy = [[position(x, y, z, 1) for x in range(NX) for y in range(NY)] for z in range(NZ)]
    return plane_xz + plane_xy


def exchange(blocks, groups):
    return lax.all_to_all(
        blocks, AXES, split_axis=0, concat_axis=0, axis_index_groups=groups, tiled=True
    )


def attend_kernel(
    lengths_ref,
    hidden_ref,
    q_ref,
    new_key_ref,
    new_value_ref,
    keys_ref,
    values_ref,
    gain_ref,
    ids_ref,
    routing_ref,
    previous_ref,
    talker_gain_ref,
    sent_ref,
    residual_ref,
    talker_ref,
):
    count, span, _ = keys_ref.shape
    width = hidden_ref.shape[1]
    group = width // HD // KVH
    scale = HD ** (-0.5)
    row = lax.broadcasted_iota(jnp.int32, (count, count * span), 0)
    offset = lax.broadcasted_iota(jnp.int32, (count, count * span), 1) - row * span
    first = lax.broadcasted_iota(jnp.int32, (count, 1), 0)
    lengths = jnp.zeros((count, 1), jnp.int32)
    for r in range(count):
        lengths = jnp.where(first == r, lengths_ref[r], lengths)
    valid = jnp.logical_and(offset >= 0, offset < lengths)
    bias = jnp.concatenate([jnp.where(valid, 0.0, -1e30)] * group, axis=0)
    square = jnp.zeros((count, HD), jnp.float32)
    heads = []
    for head in range(KVH):
        lanes = [slice((head * group + h) * HD, (head * group + h + 1) * HD) for h in range(group)]
        query = jnp.concatenate([q_ref[:, lane] for lane in lanes], axis=0)
        own_lane = slice(head * HD, (head + 1) * HD)
        keys = keys_ref[:, :, own_lane].reshape(count * span, HD)
        cached = lax.dot_general(
            query, keys, (((1,), (1,)), ((), ())), preferred_element_type=jnp.float32
        )
        cached = cached * scale + bias
        new_key = jnp.concatenate([new_key_ref[:, own_lane]] * group, axis=0).astype(jnp.float32)
        own = jnp.sum(query.astype(jnp.float32) * new_key, axis=-1, keepdims=True) * scale
        heads.append((lanes, own_lane, cached, own))
    tops = [jnp.maximum(jnp.max(c, axis=-1, keepdims=True), o) for _, _, c, o in heads]
    weights = [jnp.exp(c - t) for (_, _, c, _), t in zip(heads, tops)]
    owns = [jnp.exp(o - t) for (_, _, _, o), t in zip(heads, tops)]
    shares = [1.0 / (jnp.sum(w, axis=-1, keepdims=True) + o) for w, o in zip(weights, owns)]
    for (lanes, own_lane, _, _), weight, own_weight, share in zip(heads, weights, owns, shares):
        values = values_ref[:, :, own_lane].reshape(count * span, HD)
        probs = (weight * share).astype(jnp.bfloat16)
        own_prob = (own_weight * share).astype(jnp.bfloat16).astype(jnp.float32)
        mixed = jnp.dot(probs, values, preferred_element_type=jnp.float32)
        new_value = jnp.concatenate([new_value_ref[:, own_lane]] * group, axis=0)
        mixed = mixed + own_prob * new_value.astype(jnp.float32)
        for h, lane in enumerate(lanes):
            after = hidden_ref[:, lane].astype(jnp.float32) + mixed[h * count : (h + 1) * count]
            residual_ref[:, lane] = after
            square = square + after * after
    norm = lax.rsqrt(jnp.sum(square, axis=-1, keepdims=True) / width + 1e-06)
    gain = gain_ref[...].astype(jnp.float32).reshape(1, width)
    moe_in = (residual_ref[...] * norm * gain).astype(jnp.bfloat16)
    ids, routing = ids_ref[...], routing_ref[...].astype(jnp.float32)
    experts = sent_ref.shape[2] - width
    expert = lax.broadcasted_iota(jnp.int32, (experts, count), 0)
    route = jnp.zeros((experts, count), jnp.float32)
    for k in range(ids.shape[0]):
        route = route + jnp.where(expert == ids[k : k + 1], routing[k : k + 1], 0.0)
    route = route.T.astype(jnp.bfloat16)
    for copy in range(sent_ref.shape[0]):
        sent_ref[copy, :, :width] = moe_in
        sent_ref[copy, :, width:] = route
    previous = previous_ref[...].astype(jnp.float32)
    norm = lax.rsqrt(jnp.mean(previous * previous, axis=-1, keepdims=True) + 1e-06)
    gain = talker_gain_ref[...].astype(jnp.float32).reshape(1, width)
    talker_ref[...] = (previous * norm * gain).astype(jnp.bfloat16)


def origin(ndim, step):
    return (0,) * ndim


def attend(
    copies,
    experts,
    hidden,
    queries,
    new_keys,
    new_values,
    cache_keys,
    cache_values,
    lengths,
    gain,
    ids,
    routing,
    previous,
    talker_gain,
):
    count, width = hidden.shape
    operands = (
        hidden,
        queries,
        new_keys,
        new_values,
        cache_keys,
        cache_values,
        gain,
        ids.T,
        routing.T,
        previous,
        talker_gain,
    )
    return pl.pallas_call(
        attend_kernel,
        grid=(1,),
        in_specs=[pl.BlockSpec(memory_space=pltpu.SMEM)]
        + [pl.BlockSpec(o.shape, functools.partial(origin, o.ndim)) for o in operands],
        out_specs=[
            pl.BlockSpec((copies, count, width + experts), functools.partial(origin, 3)),
            pl.BlockSpec((count, width), functools.partial(origin, 2)),
            pl.BlockSpec((count, width), functools.partial(origin, 2)),
        ],
        out_shape=[
            pltpu.HBM((copies, count, width + experts), jnp.bfloat16),
            jax.ShapeDtypeStruct((count, width), jnp.float32),
            pltpu.HBM((count, width), jnp.bfloat16),
        ],
        compiler_params=pltpu.CompilerParams(vmem_limit_bytes=BIG_VMEM),
        name="attend",
    )(lengths, *operands)


def from_row(values, ahead):
    return lax.ppermute(values, "tk", [((y + ahead) % NY, y) for y in range(NY)])


def dispatch_kernel(where_ref, held_ref, o_ref, weight_ref, out_ref, sems):
    core, tk, z_lo = where_ref[0], where_ref[1], where_ref[2]
    width = o_ref.shape[1]
    rows, experts = weight_ref.shape[0], held_ref.shape[1] - width
    targets = NX * NZ
    slots = weight_ref.shape[1] // targets
    across = (((1,), (1,)), ((), ()))

    def count(shape, axis):
        return lax.broadcasted_iota(jnp.int32, shape, axis)

    def bits(mask):
        return mask.astype(jnp.bfloat16)

    target = count((targets, experts), 0)
    x, rest = target // NZ, target % NZ
    holds = jnp.where(core == 0, (x * NZL + rest % NZL) * NY + tk, (x * NZL + z_lo) * NY + rest)
    chosen = bits(holds == count((targets, experts), 1))
    route = held_ref[:, width:]

    share = lax.dot_general(chosen, route, across, preferred_element_type=jnp.float32)
    until = bits(count((rows, rows), 0) <= count((rows, rows), 1))
    rank = jnp.dot(bits(share > 0), until, preferred_element_type=jnp.float32)
    rank = jnp.where(share > 0, rank, 0.0)
    shape = (targets, slots, rows)
    slot = count(shape, 1).astype(jnp.float32) + 1.0
    inside = jnp.broadcast_to(rank[:, None, :], shape) == slot
    pick = bits(jnp.where(inside, 1.0, 0.0).reshape(targets * slots, rows))
    parts, _, part = out_ref.shape
    copies = []
    for i in range(parts):
        lanes = pl.ds(i * part, part)
        out = jnp.dot(pick, held_ref[:, lanes], preferred_element_type=jnp.float32)
        out_ref[i] = out.astype(jnp.bfloat16)
        copies.append(pltpu.make_async_copy(out_ref.at[i], o_ref.at[:, lanes], sems.at[i]))
        copies[-1].start()

    share = lax.dot_general(route, chosen, across, preferred_element_type=jnp.float32)
    since = bits(count((rows, rows), 0) >= count((rows, rows), 1))
    rank = jnp.dot(since, bits(share > 0), preferred_element_type=jnp.float32)
    rank = jnp.where(share > 0, rank, 0.0)
    wide = (targets, targets * slots)
    repeat = bits(count(wide, 0) == count(wide, 1) // slots)
    rank = jnp.dot(rank.astype(jnp.bfloat16), repeat, preferred_element_type=jnp.float32)
    share = jnp.dot(share.astype(jnp.bfloat16), repeat, preferred_element_type=jnp.float32)
    slot = (count(rank.shape, 1) % slots).astype(jnp.float32) + 1.0
    weight_ref[...] = jnp.where(rank == slot, share, 0.0).astype(jnp.bfloat16)
    for copy in copies:
        copy.wait()


def dispatch(held, width, slots):
    rows = held.shape[0]
    count = NX * NZ * slots
    exp, rep, tk = (lax.axis_index(a) for a in AXES)
    where = jnp.stack([rep % 2, tk, exp % NZL]).astype(jnp.int32)
    parts = 4
    return pl.pallas_call(
        dispatch_kernel,
        in_specs=[
            pl.BlockSpec(memory_space=pltpu.SMEM),
            pl.BlockSpec(memory_space=pltpu.VMEM),
        ],
        out_specs=[
            pl.BlockSpec(memory_space=pltpu.HBM),
            pl.BlockSpec(memory_space=pltpu.VMEM),
        ],
        out_shape=[
            pltpu.HBM((count, width), jnp.bfloat16),
            jax.ShapeDtypeStruct((rows, count), jnp.bfloat16),
        ],
        scratch_shapes=[
            pltpu.VMEM((parts, count, width // parts), jnp.bfloat16),
            pltpu.SemaphoreType.DMA((parts,)),
        ],
        compiler_params=pltpu.CompilerParams(vmem_limit_bytes=SMALL_VMEM),
        name="dispatch",
    )(where, held)


def pack_kernel(*refs):
    weights, (packed_ref, sems) = refs[:-2], refs[-2:]
    units = weights[0].shape[0]
    copies = [
        pltpu.make_async_copy(w, packed_ref.at[pl.ds(i * units, units)], sems.at[i])
        for i, w in enumerate(weights)
    ]
    for copy in copies:
        copy.start()
    for copy in copies:
        copy.wait()


def pack(weights):
    units, width = weights[0].shape
    count = len(weights)
    return pl.pallas_call(
        pack_kernel,
        in_specs=[pl.BlockSpec(memory_space=pl.ANY)] * count,
        out_specs=pl.BlockSpec(memory_space=pltpu.HBM),
        out_shape=pltpu.HBM((count * units, width), jnp.bfloat16),
        scratch_shapes=[pltpu.SemaphoreType.DMA((count,))],
        compiler_params=pltpu.CompilerParams(vmem_limit_bytes=SMALL_VMEM),
        cost_estimate=pl.CostEstimate(
            flops=0, bytes_accessed=4 * count * units * width, transcendentals=0
        ),
        name="pack",
    )(*weights)


def expert_kernel(x_ref, packed_ref, o_ref, active_ref, out_ref, sems):
    units = packed_ref.shape[0] // 3
    across = (((1,), (1,)), ((), ()))
    x = x_ref[...]
    gate, up = packed_ref[:units], packed_ref[units : 2 * units]
    gated = lax.dot_general(x, gate, across, preferred_element_type=jnp.float32)
    raised = lax.dot_general(x, up, across, preferred_element_type=jnp.float32)
    active_ref[...] = (gated / (1.0 + jnp.exp(-gated)) * raised).astype(jnp.bfloat16)
    parts, _, part = out_ref.shape
    copies = []
    for i in range(parts):
        lanes = pl.ds(i * part, part)
        down = packed_ref[2 * units :, lanes]
        out = jnp.dot(active_ref[...], down, preferred_element_type=jnp.float32)
        out_ref[i] = out.astype(jnp.bfloat16)
        copies.append(pltpu.make_async_copy(out_ref.at[i], o_ref.at[:, lanes], sems.at[i]))
        copies[-1].start()
    for copy in copies:
        copy.wait()


def expert_apply(rows, packed):
    count, width = rows.shape
    units = packed.shape[0] // 3
    parts = 4
    return pl.pallas_call(
        expert_kernel,
        in_specs=[pl.BlockSpec(memory_space=pltpu.VMEM)] * 2,
        out_specs=pl.BlockSpec(memory_space=pltpu.HBM),
        out_shape=pltpu.HBM((count, width), jnp.bfloat16),
        scratch_shapes=[
            pltpu.VMEM((count, units), jnp.bfloat16),
            pltpu.VMEM((parts, count, width // parts), jnp.bfloat16),
            pltpu.SemaphoreType.DMA((parts,)),
        ],
        compiler_params=pltpu.CompilerParams(vmem_limit_bytes=SMALL_VMEM),
        cost_estimate=pl.CostEstimate(
            flops=6 * count * width * units,
            bytes_accessed=4 * count * width + 6 * units * width,
            transcendentals=count * units,
        ),
        name="experts",
    )(rows, packed)


def per_device(
    hidden_input_rows,
    queries,
    new_keys,
    new_values,
    cache_keys,
    cache_values,
    cache_lengths,
    moe_gain,
    expert_ids,
    routing_weights,
    expert_gate,
    expert_up,
    expert_down,
    prev_hidden,
    talker_gain,
    talker_proj,
):
    count, width = hidden_input_rows.shape
    experts = lax.axis_size("exp") * lax.axis_size("tk")
    lines, planes = line_groups(), plane_groups()
    line = len(lines[0])

    sent, residual, talker_rows = attend(
        line,
        experts,
        hidden_input_rows,
        queries,
        new_keys,
        new_values,
        cache_keys,
        cache_values,
        cache_lengths,
        moe_gain,
        expert_ids,
        routing_weights,
        prev_hidden,
        talker_gain,
    )

    near = [from_row(talker_rows, 1), from_row(talker_rows, -1)]
    held = exchange(sent, lines).reshape(line * count, width + experts)
    held, near = lax.optimization_barrier((held, near))
    slots = 2 * line
    outgoing, weight = dispatch(held, width, slots)

    own = [w[0].T for w in (expert_gate, expert_up, expert_down)]
    outgoing, own, near = lax.optimization_barrier((outgoing, own, near))
    other = [lax.ppermute(w, "rep", [(r, r ^ 1) for r in range(2 * NZH)]) for w in own]
    second = [from_row(near[0], 1), from_row(near[1], -1)]
    arrived = exchange(outgoing.reshape(-1, slots, width), planes).reshape(-1, width)
    packed = pack([own[0], other[0], own[1], other[1], own[2], other[2]])
    arrived, packed, second = lax.optimization_barrier((arrived, packed, second))
    computed = expert_apply(arrived, packed)

    computed, second = lax.optimization_barrier((computed, second))
    third = [from_row(second[0], 1), from_row(second[1], -1)]
    half = count // 2
    third += [from_row(second[0][:half], 2), from_row(second[1][half:], -2)]
    returned = exchange(computed.reshape(-1, slots, width), planes).reshape(-1, width)
    returned, third = lax.optimization_barrier((returned, third))
    partial_rows = jnp.dot(weight, returned, preferred_element_type=jnp.float32)
    partial_rows = partial_rows.astype(jnp.bfloat16)
    partial_rows, third = lax.optimization_barrier((partial_rows, third))
    pieces = exchange(partial_rows.reshape(line, count, width), lines)
    layer_out = (residual + jnp.sum(pieces.astype(jnp.float32), axis=0)).astype(jnp.bfloat16)

    ahead = [talker_rows, near[0], second[0], third[0], third[2], third[3]]
    gathered = jnp.concatenate(ahead + [third[1], second[1], near[1]], axis=0)
    talker_in = jnp.dot(gathered, talker_proj, preferred_element_type=jnp.float32)
    talker_in = talker_in.astype(jnp.bfloat16)
    start = (NY - lax.axis_index("tk")) * count
    talker_in = lax.dynamic_slice_in_dim(
        jnp.concatenate([talker_in, talker_in], axis=0), start, NY * count, axis=0
    )
    return (layer_out, talker_in)


def solution(mesh):
    placed = (
        P(("exp", "rep", "tk"), None),
        P(("exp", "rep", "tk"), None),
        P(("exp", "rep", "tk"), None),
        P(("exp", "rep", "tk"), None),
        P(("exp", "rep", "tk"), None, None),
        P(("exp", "rep", "tk"), None, None),
        P(("exp", "rep", "tk")),
        P(),
        P(("exp", "rep", "tk"), None),
        P(("exp", "rep", "tk"), None),
        P(("exp", "tk"), None, "rep"),
        P(("exp", "tk"), None, "rep"),
        P(("exp", "tk"), None, "rep"),
        P(("exp", "rep", "tk"), None),
        P(),
        P(None, "tk"),
    )
    return jax.shard_map(
        per_device,
        mesh=mesh,
        in_specs=placed,
        out_specs=(P(("exp", "rep", "tk"), None), P(("exp", "rep"), "tk")),
        check_vma=False,
    )
```

```python
import functools

import jax
import jax.numpy as jnp
from jax import lax
from jax.experimental import pallas as pl
from jax.experimental.pallas import tpu as pltpu
from jax.sharding import PartitionSpec as P

HD = 128
KVH = 4
BIG_VMEM = 61 * 1024 * 1024
SMALL_VMEM = 12 * 1024 * 1024
AXES = ("exp", "rep", "tk")
NX, NZL, NZH, NY = 4, 4, 2, 8
NZ = NZL * NZH


def position(x, y, z, core):
    return ((x * NZL + z % NZL) * 2 * NZH + (z // NZL) * 2 + core) * NY + y


def line_groups():
    along_y = [[position(x, y, z, 0) for y in range(NY)] for x in range(NX) for z in range(NZ)]
    along_z = [[position(x, y, z, 1) for z in range(NZ)] for x in range(NX) for y in range(NY)]
    return along_y + along_z


def plane_groups():
    plane_xz = [[position(x, y, z, 0) for x in range(NX) for z in range(NZ)] for y in range(NY)]
    plane_xy = [[position(x, y, z, 1) for x in range(NX) for y in range(NY)] for z in range(NZ)]
    return plane_xz + plane_xy


def exchange(blocks, groups):
    return lax.all_to_all(
        blocks, AXES, split_axis=0, concat_axis=0, axis_index_groups=groups, tiled=True
    )


def attend_kernel(
    lengths_ref,
    hidden_ref,
    q_ref,
    new_key_ref,
    new_value_ref,
    keys_ref,
    values_ref,
    gain_ref,
    ids_ref,
    routing_ref,
    previous_ref,
    talker_gain_ref,
    sent_ref,
    residual_ref,
    talker_ref,
):
    count, span, _ = keys_ref.shape
    width = hidden_ref.shape[1]
    group = width // HD // KVH
    scale = HD ** (-0.5)
    row = lax.broadcasted_iota(jnp.int32, (count, count * span), 0)
    offset = lax.broadcasted_iota(jnp.int32, (count, count * span), 1) - row * span
    first = lax.broadcasted_iota(jnp.int32, (count, 1), 0)
    lengths = jnp.zeros((count, 1), jnp.int32)
    for r in range(count):
        lengths = jnp.where(first == r, lengths_ref[r], lengths)
    valid = jnp.logical_and(offset >= 0, offset < lengths)
    bias = jnp.concatenate([jnp.where(valid, 0.0, -1e30)] * group, axis=0)
    square = jnp.zeros((count, HD), jnp.float32)
    heads = []
    for head in range(KVH):
        lanes = [slice((head * group + h) * HD, (head * group + h + 1) * HD) for h in range(group)]
        query = jnp.concatenate([q_ref[:, lane] for lane in lanes], axis=0)
        own_lane = slice(head * HD, (head + 1) * HD)
        keys = keys_ref[:, :, own_lane].reshape(count * span, HD)
        cached = lax.dot_general(
            query, keys, (((1,), (1,)), ((), ())), preferred_element_type=jnp.float32
        )
        cached = cached * scale + bias
        new_key = jnp.concatenate([new_key_ref[:, own_lane]] * group, axis=0).astype(jnp.float32)
        own = jnp.sum(query.astype(jnp.float32) * new_key, axis=-1, keepdims=True) * scale
        heads.append((lanes, own_lane, cached, own))
    tops = [jnp.maximum(jnp.max(c, axis=-1, keepdims=True), o) for _, _, c, o in heads]
    weights = [jnp.exp(c - t) for (_, _, c, _), t in zip(heads, tops)]
    owns = [jnp.exp(o - t) for (_, _, _, o), t in zip(heads, tops)]
    shares = [1.0 / (jnp.sum(w, axis=-1, keepdims=True) + o) for w, o in zip(weights, owns)]
    for (lanes, own_lane, _, _), weight, own_weight, share in zip(heads, weights, owns, shares):
        values = values_ref[:, :, own_lane].reshape(count * span, HD)
        probs = (weight * share).astype(jnp.bfloat16)
        own_prob = (own_weight * share).astype(jnp.bfloat16).astype(jnp.float32)
        mixed = jnp.dot(probs, values, preferred_element_type=jnp.float32)
        new_value = jnp.concatenate([new_value_ref[:, own_lane]] * group, axis=0)
        mixed = mixed + own_prob * new_value.astype(jnp.float32)
        for h, lane in enumerate(lanes):
            after = hidden_ref[:, lane].astype(jnp.float32) + mixed[h * count : (h + 1) * count]
            residual_ref[:, lane] = after
            square = square + after * after
    norm = lax.rsqrt(jnp.sum(square, axis=-1, keepdims=True) / width + 1e-06)
    gain = gain_ref[...].astype(jnp.float32).reshape(1, width)
    moe_in = (residual_ref[...] * norm * gain).astype(jnp.bfloat16)
    ids, routing = ids_ref[...], routing_ref[...].astype(jnp.float32)
    experts = sent_ref.shape[2] - width
    expert = lax.broadcasted_iota(jnp.int32, (experts, count), 0)
    route = jnp.zeros((experts, count), jnp.float32)
    for k in range(ids.shape[0]):
        route = route + jnp.where(expert == ids[k : k + 1], routing[k : k + 1], 0.0)
    route = route.T.astype(jnp.bfloat16)
    for copy in range(sent_ref.shape[0]):
        sent_ref[copy, :, :width] = moe_in
        sent_ref[copy, :, width:] = route
    previous = previous_ref[...].astype(jnp.float32)
    norm = lax.rsqrt(jnp.mean(previous * previous, axis=-1, keepdims=True) + 1e-06)
    gain = talker_gain_ref[...].astype(jnp.float32).reshape(1, width)
    talker_ref[...] = (previous * norm * gain).astype(jnp.bfloat16)


def origin(ndim, step):
    return (0,) * ndim


def attend(
    copies,
    experts,
    hidden,
    queries,
    new_keys,
    new_values,
    cache_keys,
    cache_values,
    lengths,
    gain,
    ids,
    routing,
    previous,
    talker_gain,
):
    count, width = hidden.shape
    operands = (
        hidden,
        queries,
        new_keys,
        new_values,
        cache_keys,
        cache_values,
        gain,
        ids.T,
        routing.T,
        previous,
        talker_gain,
    )
    return pl.pallas_call(
        attend_kernel,
        grid=(1,),
        in_specs=[pl.BlockSpec(memory_space=pltpu.SMEM)]
        + [pl.BlockSpec(o.shape, functools.partial(origin, o.ndim)) for o in operands],
        out_specs=[
            pl.BlockSpec((copies, count, width + experts), functools.partial(origin, 3)),
            pl.BlockSpec((count, width), functools.partial(origin, 2)),
            pl.BlockSpec((count, width), functools.partial(origin, 2)),
        ],
        out_shape=[
            pltpu.HBM((copies, count, width + experts), jnp.bfloat16),
            jax.ShapeDtypeStruct((count, width), jnp.float32),
            pltpu.HBM((count, width), jnp.bfloat16),
        ],
        compiler_params=pltpu.CompilerParams(vmem_limit_bytes=BIG_VMEM),
        name="attend",
    )(lengths, *operands)


def from_row(values, ahead):
    return lax.ppermute(values, "tk", [((y + ahead) % NY, y) for y in range(NY)])


def dispatch_kernel(where_ref, held_ref, o_ref, weight_ref, out_ref, sems):
    core, tk, z_lo = where_ref[0], where_ref[1], where_ref[2]
    width = o_ref.shape[1]
    rows, experts = weight_ref.shape[0], held_ref.shape[1] - width
    targets = NX * NZ
    slots = weight_ref.shape[1] // targets
    across = (((1,), (1,)), ((), ()))

    def count(shape, axis):
        return lax.broadcasted_iota(jnp.int32, shape, axis)

    def bits(mask):
        return mask.astype(jnp.bfloat16)

    target = count((targets, experts), 0)
    x, rest = target // NZ, target % NZ
    holds = jnp.where(core == 0, (x * NZL + rest % NZL) * NY + tk, (x * NZL + z_lo) * NY + rest)
    chosen = bits(holds == count((targets, experts), 1))
    route = held_ref[:, width:]

    share = lax.dot_general(chosen, route, across, preferred_element_type=jnp.float32)
    until = bits(count((rows, rows), 0) <= count((rows, rows), 1))
    rank = jnp.dot(bits(share > 0), until, preferred_element_type=jnp.float32)
    rank = jnp.where(share > 0, rank, 0.0)
    shape = (targets, slots, rows)
    slot = count(shape, 1).astype(jnp.float32) + 1.0
    inside = jnp.broadcast_to(rank[:, None, :], shape) == slot
    pick = bits(jnp.where(inside, 1.0, 0.0).reshape(targets * slots, rows))
    parts, _, part = out_ref.shape
    copies = []
    for i in range(parts):
        lanes = pl.ds(i * part, part)
        out = jnp.dot(pick, held_ref[:, lanes], preferred_element_type=jnp.float32)
        out_ref[i] = out.astype(jnp.bfloat16)
        copies.append(pltpu.make_async_copy(out_ref.at[i], o_ref.at[:, lanes], sems.at[i]))
        copies[-1].start()

    share = lax.dot_general(route, chosen, across, preferred_element_type=jnp.float32)
    since = bits(count((rows, rows), 0) >= count((rows, rows), 1))
    rank = jnp.dot(since, bits(share > 0), preferred_element_type=jnp.float32)
    rank = jnp.where(share > 0, rank, 0.0)
    wide = (targets, targets * slots)
    repeat = bits(count(wide, 0) == count(wide, 1) // slots)
    rank = jnp.dot(rank.astype(jnp.bfloat16), repeat, preferred_element_type=jnp.float32)
    share = jnp.dot(share.astype(jnp.bfloat16), repeat, preferred_element_type=jnp.float32)
    slot = (count(rank.shape, 1) % slots).astype(jnp.float32) + 1.0
    weight_ref[...] = jnp.where(rank == slot, share, 0.0).astype(jnp.bfloat16)
    for copy in copies:
        copy.wait()


def dispatch(held, width, slots):
    rows = held.shape[0]
    count = NX * NZ * slots
    exp, rep, tk = (lax.axis_index(a) for a in AXES)
    where = jnp.stack([rep % 2, tk, exp % NZL]).astype(jnp.int32)
    parts = 4
    return pl.pallas_call(
        dispatch_kernel,
        in_specs=[
            pl.BlockSpec(memory_space=pltpu.SMEM),
            pl.BlockSpec(memory_space=pltpu.VMEM),
        ],
        out_specs=[
            pl.BlockSpec(memory_space=pltpu.HBM),
            pl.BlockSpec(memory_space=pltpu.VMEM),
        ],
        out_shape=[
            pltpu.HBM((count, width), jnp.bfloat16),
            jax.ShapeDtypeStruct((rows, count), jnp.bfloat16),
        ],
        scratch_shapes=[
            pltpu.VMEM((parts, count, width // parts), jnp.bfloat16),
            pltpu.SemaphoreType.DMA((parts,)),
        ],
        compiler_params=pltpu.CompilerParams(vmem_limit_bytes=SMALL_VMEM),
        name="dispatch",
    )(where, held)


def pack_kernel(*refs):
    weights, (packed_ref, sems) = refs[:-2], refs[-2:]
    units = weights[0].shape[0]
    copies = [
        pltpu.make_async_copy(w, packed_ref.at[pl.ds(i * units, units)], sems.at[i])
        for i, w in enumerate(weights)
    ]
    for copy in copies:
        copy.start()
    for copy in copies:
        copy.wait()


def pack(weights):
    units, width = weights[0].shape
    count = len(weights)
    return pl.pallas_call(
        pack_kernel,
        in_specs=[pl.BlockSpec(memory_space=pl.ANY)] * count,
        out_specs=pl.BlockSpec(memory_space=pltpu.HBM),
        out_shape=pltpu.HBM((count * units, width), jnp.bfloat16),
        scratch_shapes=[pltpu.SemaphoreType.DMA((count,))],
        compiler_params=pltpu.CompilerParams(vmem_limit_bytes=SMALL_VMEM),
        cost_estimate=pl.CostEstimate(
            flops=0, bytes_accessed=4 * count * units * width, transcendentals=0
        ),
        name="pack",
    )(*weights)


def expert_kernel(x_ref, packed_ref, o_ref, active_ref, out_ref, sems):
    units = packed_ref.shape[0] // 3
    across = (((1,), (1,)), ((), ()))
    x = x_ref[...]
    gate, up = packed_ref[:units], packed_ref[units : 2 * units]
    gated = lax.dot_general(x, gate, across, preferred_element_type=jnp.float32)
    raised = lax.dot_general(x, up, across, preferred_element_type=jnp.float32)
    active_ref[...] = (gated / (1.0 + jnp.exp(-gated)) * raised).astype(jnp.bfloat16)
    parts, _, part = out_ref.shape
    copies = []
    for i in range(parts):
        lanes = pl.ds(i * part, part)
        down = packed_ref[2 * units :, lanes]
        out = jnp.dot(active_ref[...], down, preferred_element_type=jnp.float32)
        out_ref[i] = out.astype(jnp.bfloat16)
        copies.append(pltpu.make_async_copy(out_ref.at[i], o_ref.at[:, lanes], sems.at[i]))
        copies[-1].start()
    for copy in copies:
        copy.wait()


def expert_apply(rows, packed):
    count, width = rows.shape
    units = packed.shape[0] // 3
    parts = 4
    return pl.pallas_call(
        expert_kernel,
        in_specs=[pl.BlockSpec(memory_space=pltpu.VMEM)] * 2,
        out_specs=pl.BlockSpec(memory_space=pltpu.HBM),
        out_shape=pltpu.HBM((count, width), jnp.bfloat16),
        scratch_shapes=[
            pltpu.VMEM((count, units), jnp.bfloat16),
            pltpu.VMEM((parts, count, width // parts), jnp.bfloat16),
            pltpu.SemaphoreType.DMA((parts,)),
        ],
        compiler_params=pltpu.CompilerParams(vmem_limit_bytes=SMALL_VMEM),
        cost_estimate=pl.CostEstimate(
            flops=6 * count * width * units,
            bytes_accessed=4 * count * width + 6 * units * width,
            transcendentals=count * units,
        ),
        name="experts",
    )(rows, packed)


def per_device(
    hidden_input_rows,
    queries,
    new_keys,
    new_values,
    cache_keys,
    cache_values,
    cache_lengths,
    moe_gain,
    expert_ids,
    routing_weights,
    expert_gate,
    expert_up,
    expert_down,
    prev_hidden,
    talker_gain,
    talker_proj,
):
    count, width = hidden_input_rows.shape
    experts = lax.axis_size("exp") * lax.axis_size("tk")
    lines, planes = line_groups(), plane_groups()
    line = len(lines[0])

    sent, residual, talker_rows = attend(
        line,
        experts,
        hidden_input_rows,
        queries,
        new_keys,
        new_values,
        cache_keys,
        cache_values,
        cache_lengths,
        moe_gain,
        expert_ids,
        routing_weights,
        prev_hidden,
        talker_gain,
    )

    near = [from_row(talker_rows, 1), from_row(talker_rows, -1)]
    held = exchange(sent, lines).reshape(line * count, width + experts)
    slots = 2 * line
    outgoing, weight = dispatch(held, width, slots)

    own = [w[0].T for w in (expert_gate, expert_up, expert_down)]
    outgoing, own, near = lax.optimization_barrier((outgoing, own, near))
    other = [lax.ppermute(w, "rep", [(r, r ^ 1) for r in range(2 * NZH)]) for w in own]
    second = [from_row(near[0], 1), from_row(near[1], -1)]
    arrived = exchange(outgoing.reshape(-1, slots, width), planes).reshape(-1, width)
    packed = pack([own[0], other[0], own[1], other[1], own[2], other[2]])
    arrived, packed = lax.optimization_barrier((arrived, packed))
    computed = expert_apply(arrived, packed)

    computed, second = lax.optimization_barrier((computed, second))
    third = [from_row(second[0], 1), from_row(second[1], -1)]
    half = count // 2
    third += [from_row(second[0][:half], 2), from_row(second[1][half:], -2)]
    returned = exchange(computed.reshape(-1, slots, width), planes).reshape(-1, width)
    partial_rows = jnp.dot(weight, returned, preferred_element_type=jnp.float32)
    partial_rows = partial_rows.astype(jnp.bfloat16)
    partial_rows, third = lax.optimization_barrier((partial_rows, third))
    pieces = exchange(partial_rows.reshape(line, count, width), lines)
    layer_out = (residual + jnp.sum(pieces.astype(jnp.float32), axis=0)).astype(jnp.bfloat16)

    ahead = [talker_rows, near[0], second[0], third[0], third[2], third[3]]
    gathered = jnp.concatenate(ahead + [third[1], second[1], near[1]], axis=0)
    talker_in = jnp.dot(gathered, talker_proj, preferred_element_type=jnp.float32)
    talker_in = talker_in.astype(jnp.bfloat16)
    start = (NY - lax.axis_index("tk")) * count
    talker_in = lax.dynamic_slice_in_dim(
        jnp.concatenate([talker_in, talker_in], axis=0), start, NY * count, axis=0
    )
    return (layer_out, talker_in)


def solution(mesh):
    placed = (
        P(("exp", "rep", "tk"), None),
        P(("exp", "rep", "tk"), None),
        P(("exp", "rep", "tk"), None),
        P(("exp", "rep", "tk"), None),
        P(("exp", "rep", "tk"), None, None),
        P(("exp", "rep", "tk"), None, None),
        P(("exp", "rep", "tk")),
        P(),
        P(("exp", "rep", "tk"), None),
        P(("exp", "rep", "tk"), None),
        P(("exp", "tk"), None, "rep"),
        P(("exp", "tk"), None, "rep"),
        P(("exp", "tk"), None, "rep"),
        P(("exp", "rep", "tk"), None),
        P(),
        P(None, "tk"),
    )
    return jax.shard_map(
        per_device,
        mesh=mesh,
        in_specs=placed,
        out_specs=(P(("exp", "rep", "tk"), None), P(("exp", "rep"), "tk")),
        check_vma=False,
    )
```
